256 devices in a mesh: section: 16 (over y, x_hi, core), seq: 16 (over z, x_lo).
Axes of the slice: x: 4 (x_hi: 2, x_lo: 2; x = x_hi * 2 + x_lo), y: 4, z: 8, core: 2. Of those that a mesh axis runs over, the one named last changes fastest.
Arguments:
- latent: bfloat16 [4, 384, 3072], P(None, 'seq'), may hold values from -6 to 6
- in_flight: bfloat16 [16, 384, 3072], P('section', 'seq'), may hold values from -9 to 9
- patch_order: int32 [4], replicated, may hold values from 0 to 3, each once
- w_qkv: bfloat16 [16, 3072, 3, 4096], P('section', None, None, 'seq'), may hold values from -0.109375 to 0.109375
- w_out: bfloat16 [16, 4096, 3072], P('section', 'seq'), may hold values from -0.375 to 0.375
- stale_kv: bfloat16 [16, 4, 384, 2, 4096], P('section', None, None, None, 'seq'), may hold values from -6 to 6
- mod_shift: float32 [16, 3072], P('section'), may hold values from -3 to 3
- mod_scale: float32 [16, 3072], P('section'), may hold values from -0.5 to 0.5
- mod_gate: float32 [16, 3072], P('section'), may hold values from 0.5 to 1.5
- q_gain: float32 [16, 32, 128], P('section', 'seq'), may hold values from 1 to 3
Outputs:
- block_out: bfloat16 [16, 4, 384, 3072], P('section', None, 'seq')
- new_kv: bfloat16 [16, 4, 384, 2, 4096], P('section', None, None, None, 'seq')
The draws below stay inside these ranges and needn't reach their ends.
Inputs may be any that keep to these rules, and one draw needn't show every extreme that they name: `patch_order`: a permutation of the 4 patch numbers.
All inputs are finite; a program needn't handle non-finite values.
Results may differ from the reference program's by a relative error of at most 0.028.
Values may be sent and summed in bfloat16 or wider, within the bound.
No kernel may reach another device: no remote copies, remote signals or barrier semaphores. Data moves between devices by JAX's collectives and lax.ppermute only.
A program may use at most 128 MiB of HBM per device.

```python
import math
import jax
import jax.numpy as jnp
from jax import lax

D = 3072
HEADS = 32
HD = 128
PATCHES = 4
PATCH_TOK = 384
N_SECTION = 16
N_SEQ = 16


def shard_levels(key, extent, pieces, low, top_value):
    level, own = 1.0, jax.random.fold_in(key, 6)
    for position, blocks in pieces:
        steps = jnp.exp(jax.random.uniform(jax.random.fold_in(own, position), (blocks,), jnp.float32, low / len(pieces), top_value / len(pieces)))
        level = level * jnp.repeat(steps, extent[position] // blocks).reshape([-1 if axis == position else 1 for axis in range(len(extent))])
    return level


def scatter_about(rng, extent, scale, bound, shards=(), kind=jnp.bfloat16):
    loudness = shard_levels(rng, extent, shards, -0.22, 0.18) if shards else 1.0
    array = jax.random.normal(rng, extent, jnp.float32) * scale * loudness
    return jnp.minimum(jnp.maximum(array, -bound), bound).astype(kind)


def setup_inputs(seed: int = 0) -> dict:
    keys = jax.random.split(jax.random.key(seed), 11)
    latent = scatter_about(keys[0], (PATCHES, PATCH_TOK, D), 1.0, 6.0, ((1, 16),))
    in_flight = scatter_about(keys[1], (N_SECTION, PATCH_TOK, D), 1.5, 9.0, ((0, 16), (1, 16)))
    patch_order = jax.random.permutation(keys[2], PATCHES).astype(jnp.int32)
    w_qkv = scatter_about(keys[3], (N_SECTION, D, 3, HEADS * HD), D ** -0.5, 0.109375, ((0, 16), (3, 16)))
    w_out = scatter_about(keys[4], (N_SECTION, HEADS * HD, D), (2 * HD) ** -0.5, 0.375, ((0, 16), (1, 16)))
    stale_kv = scatter_about(keys[5], (N_SECTION, PATCHES, PATCH_TOK, 2, HEADS * HD), 1.0, 6.0, ((0, 16), (4, 16)))
    mod_shift = scatter_about(keys[6], (N_SECTION, D), 0.5, 3.0, ((0, 16),), jnp.float32)
    mod_scale = jnp.clip(jax.random.uniform(keys[7], (N_SECTION, D), jnp.float32, -0.5, 0.5) * shard_levels(keys[7], (N_SECTION, D), ((0, 16),), -0.4, 0.0), -0.5, 0.5)
    mod_gate = jnp.clip(0.5 + 1.0 * jax.random.uniform(keys[8], (N_SECTION, D), jnp.float32) ** shard_levels(keys[8], (N_SECTION, D), ((0, 16),), -0.2, 0.2), 0.5, 1.5)
    q_gain = jnp.clip(jnp.exp(math.log(3.0) - 1.0986123 * jax.random.uniform(keys[9], (N_SECTION, HEADS, HD), jnp.float32) ** shard_levels(keys[9], (N_SECTION, HEADS, HD), ((0, 16), (1, 16)), -0.2, 0.2)), 1.0, 3.0)
    return dict(latent=latent, in_flight=in_flight, patch_order=patch_order, w_qkv=w_qkv, w_out=w_out, stale_kv=stale_kv, mod_shift=mod_shift, mod_scale=mod_scale, mod_gate=mod_gate, q_gain=q_gain)


def unit_rms(values):
    return values * lax.rsqrt(lax.optimization_barrier(jnp.mean(values * values, axis=-1, keepdims=True)) + 1e-06)

def modulate(hidden, shift_row, scale_row):
    floats = hidden.astype(jnp.float32)
    centred = floats - lax.optimization_barrier(jnp.mean(floats, axis=-1, keepdims=True))
    spread = lax.optimization_barrier(jnp.mean(centred * centred, axis=-1, keepdims=True))
    return (centred * lax.rsqrt(spread + 1e-06) * (1.0 + scale_row) + shift_row).astype(jnp.bfloat16)

def attend(queries, key_norms, kv_state, gain_rows):
    patch_rows = queries.shape[0]
    head_count, head_size = gain_rows.shape
    query_norm = (unit_rms(queries.reshape(patch_rows, head_count, head_size)) * gain_rows).astype(jnp.bfloat16)
    total_keys = kv_state.shape[0] * kv_state.shape[1]
    key_rows = key_norms.reshape(total_keys, head_count, head_size)
    value_rows = kv_state[:, :, 1].reshape(total_keys, head_count, head_size)
    scores = jnp.einsum('qhd,khd->hqk', query_norm.astype(jnp.float32), key_rows.astype(jnp.float32)) / math.sqrt(head_size)
    exponent = jnp.exp(scores)
    weights = (exponent / lax.optimization_barrier(jnp.sum(exponent, axis=-1, keepdims=True))).astype(jnp.bfloat16)
    blended = jnp.einsum('hqk,khd->qhd', weights.astype(jnp.float32), value_rows.astype(jnp.float32))
    return blended.astype(jnp.bfloat16).reshape(patch_rows, head_count * head_size)

def reference(latent, in_flight, patch_order, w_qkv, w_out, stale_kv, mod_shift, mod_scale, mod_gate, q_gain):
    patch_count, patch_rows, model_width = latent.shape
    inner = w_out.shape[1]
    head_count, head_size = (q_gain.shape[1], q_gain.shape[2])
    group_cols = inner // N_SEQ
    block_list = []
    state_list = []
    earlier = []
    for section_id in range(N_SECTION):
        kv_state = stale_kv[section_id]
        key_norms = unit_rms(kv_state[:, :, 0].astype(jnp.float32).reshape(patch_count, patch_rows, head_count, head_size)).astype(jnp.bfloat16)
        produced = jnp.zeros((patch_count, patch_rows, model_width), jnp.bfloat16)
        current = []
        proj_weight = w_qkv[section_id].reshape(model_width, 3 * inner)
        for wave_index in range(patch_count):
            patch_index = patch_order[(wave_index - section_id) % patch_count].astype(jnp.int32)
            if section_id == 0:
                hidden = lax.dynamic_index_in_dim(latent, patch_index, 0, keepdims=False)
            elif wave_index == 0:
                hidden = in_flight[section_id]
            else:
                hidden = earlier[wave_index - 1]
            normed = modulate(hidden, mod_shift[section_id], mod_scale[section_id])
            projected = jnp.dot(normed, proj_weight, preferred_element_type=jnp.float32)
            fresh_kv = lax.optimization_barrier(projected[:, inner:].reshape(patch_rows, 2, inner).astype(jnp.bfloat16))
            kv_state = lax.dynamic_update_index_in_dim(kv_state, fresh_kv, patch_index, 0)
            fresh_norm = unit_rms(fresh_kv[:, 0].astype(jnp.float32).reshape(patch_rows, head_count, head_size)).astype(jnp.bfloat16)
            key_norms = lax.dynamic_update_index_in_dim(key_norms, fresh_norm, patch_index, 0)
            blended = attend(projected[:, :inner], key_norms, kv_state, q_gain[section_id])
            partials = jnp.einsum('qgc,gcd->gqd', blended.reshape(patch_rows, N_SEQ, group_cols).astype(jnp.float32), w_out[section_id].reshape(N_SEQ, group_cols, model_width).astype(jnp.float32))
            rounded = lax.optimization_barrier(partials.astype(jnp.bfloat16))
            summed = lax.optimization_barrier(jnp.sum(rounded.astype(jnp.float32), axis=0))
            result = (hidden.astype(jnp.float32) + mod_gate[section_id] * summed).astype(jnp.bfloat16)
            produced = lax.dynamic_update_index_in_dim(produced, result, patch_index, 0)
            current.append(result)
        earlier = current
        block_list.append(produced)
        state_list.append(kv_state)
    return (jnp.stack(block_list), jnp.stack(state_list))
```

```python
import functools
import math

import jax
import jax.numpy as jnp
from jax import lax
from jax.experimental import pallas as pl
from jax.experimental.pallas import tpu as pltpu
from jax.sharding import PartitionSpec as P

QUAD = 4


def permute_seq(values, target):
    peers = lax.axis_size("seq")
    return lax.ppermute(values, "seq", [(i, target(i) % peers) for i in range(peers)])


VMEM = pl.BlockSpec(memory_space=pltpu.VMEM)
SMEM = pl.BlockSpec(memory_space=pltpu.SMEM)
LIMIT = 56 * 1024 * 1024


def call(kernel, outs, operands, scratch=(), scalars=0, flops=0):
    bytes_accessed = sum(v.size * v.dtype.itemsize for v in tuple(operands) + tuple(outs))
    return pl.pallas_call(
        kernel,
        out_shape=outs,
        in_specs=[SMEM] * scalars + [VMEM] * (len(operands) - scalars),
        out_specs=[VMEM] * len(outs),
        scratch_shapes=list(scratch),
        compiler_params=pltpu.CompilerParams(vmem_limit_bytes=LIMIT),
        cost_estimate=pl.CostEstimate(
            flops=flops, bytes_accessed=bytes_accessed, transcendentals=0
        ),
    )(*operands)


def modulate_kernel(hidden_ref, shift_ref, scale_ref, out_ref):
    floats = hidden_ref[...].astype(jnp.float32)
    centred = floats - jnp.mean(floats, axis=-1, keepdims=True)
    spread = jnp.mean(centred * centred, axis=-1, keepdims=True)
    out_ref[...] = (
        centred * lax.rsqrt(spread + 1e-06) * (1.0 + scale_ref[...]) + shift_ref[...]
    ).astype(jnp.bfloat16)


def modulate(hidden, shift_row, scale_row):
    outs = [jax.ShapeDtypeStruct(hidden.shape, jnp.bfloat16)]
    return call(modulate_kernel, outs, (hidden, shift_row[None], scale_row[None]))[0]


def head_norms(values, head_size):
    normed = []
    for start in range(0, values.shape[1], head_size):
        head = values[:, start : start + head_size]
        mean = jnp.mean(head * head, axis=-1, keepdims=True)
        normed.append(head * lax.rsqrt(mean + 1e-06))
    return normed


def stale_kernel(keys_ref, out_ref, *, head_size):
    for slot in range(keys_ref.shape[0]):
        heads = head_norms(keys_ref[slot].astype(jnp.float32), head_size)
        for head, normed in enumerate(heads):
            cols = slice(head * head_size, (head + 1) * head_size)
            out_ref[slot, :, cols] = normed.astype(jnp.bfloat16)


def block_kernel(
    place_ref,
    tokens_ref,
    weight_ref,
    gain_ref,
    norms_ref,
    values_ref,
    mixed_ref,
    fresh_key_ref,
    norms_out_ref,
    values_out_ref,
    order_ref,
    *,
    head_size,
    shard_rows,
    query_rows,
):
    slots, rows, cols = norms_ref.shape
    heads = cols // head_size
    half = rows // shard_rows // 2
    slot = place_ref[0]
    depth = place_ref[1]
    column = place_ref[2]
    norms_out_ref[...] = norms_ref[...]
    values_out_ref[...] = values_ref[...]
    for part in range(3):
        part_cols = slice(part * cols, (part + 1) * cols)
        product = jnp.dot(
            tokens_ref[...], weight_ref[:, part_cols], preferred_element_type=jnp.float32
        )
        for behind in range(half):
            line = lax.rem(depth - behind + half, half)
            for side in range(2):
                block = 2 * line + (column if side == 0 else 1 - column)
                start = pl.multiple_of(block * shard_rows, 8)
                piece = (2 * behind + side) * shard_rows
                order_ref[pl.ds(start, shard_rows), part_cols] = product[
                    piece : piece + shard_rows
                ]
    fresh_key = order_ref[:, cols : 2 * cols].astype(jnp.bfloat16)
    fresh_key_ref[...] = fresh_key
    key_heads = head_norms(fresh_key.astype(jnp.float32), head_size)
    for head, normed in enumerate(key_heads):
        head_cols = slice(head * head_size, (head + 1) * head_size)
        norms_out_ref[slot, :, head_cols] = normed.astype(jnp.bfloat16)
    values_out_ref[slot] = order_ref[:, 2 * cols :].astype(jnp.bfloat16)
    fold = math.log2(math.e) / math.sqrt(head_size)
    for head in range(heads):
        head_cols = slice(head * head_size, (head + 1) * head_size)
        keys = norms_out_ref[:, :, head_cols].reshape(slots * rows, head_size)
        values = values_out_ref[:, :, head_cols].reshape(slots * rows, head_size)
        for start in range(0, rows, query_rows):
            here = slice(start, start + query_rows)
            (query,) = head_norms(order_ref[here, head_cols], head_size)
            query = (query * (gain_ref[:, head_cols] * fold)).astype(jnp.bfloat16)
            scores = lax.dot_general(
                query, keys, (((1,), (1,)), ((), ())), preferred_element_type=jnp.float32
            )
            exponent = jnp.exp2(scores)
            total = jnp.sum(exponent, axis=-1, keepdims=True)
            mixed = jnp.dot(
                exponent.astype(jnp.bfloat16), values, preferred_element_type=jnp.float32
            )
            mixed_ref[here, head_cols] = (mixed / total).astype(jnp.bfloat16)


def out_kernel(*refs):
    pieces, weights, out_ref = refs[: len(refs) // 2], refs[len(refs) // 2 : -1], refs[-1]
    total = None
    for piece, weight in zip(pieces, weights):
        term = jnp.dot(piece[...], weight[...], preferred_element_type=jnp.float32)
        total = term if total is None else total + term
    out_ref[...] = total.astype(jnp.bfloat16)


def join_kernel(terms_ref, hidden_ref, gate_ref, out_ref):
    senders, rows, width = terms_ref.shape
    for place in range(QUAD):
        cols = slice(place * width, (place + 1) * width)
        total = None
        for first in range(0, senders, QUAD):
            term = terms_ref[first + place].astype(jnp.float32)
            total = term if total is None else total + term
        out_ref[:, cols] = (
            hidden_ref[:, cols].astype(jnp.float32) + gate_ref[:, cols] * total
        ).astype(jnp.bfloat16)


def gather_tokens(own):
    half = lax.axis_size("seq") // 2
    pieces = [None] * half
    pieces[0] = own
    ahead = behind = own
    for step in range(1, half // 2 + 1):
        behind = permute_seq(behind, lambda i: i + 2)
        pieces[step] = behind
        if step < half - step:
            ahead = permute_seq(ahead, lambda i: i - 2)
            pieces[half - step] = ahead
    return [(piece, permute_seq(piece, lambda i: i ^ 1)) for piece in pieces]


def shards(
    latent, in_flight, patch_order, w_qkv, w_out, stale_kv, mod_shift, mod_scale, mod_gate, q_gain
):
    patch_count, shard_rows, model_width = latent.shape
    section_index = lax.axis_index("section")
    seq_index = lax.axis_index("seq")
    seq_size = lax.axis_size("seq")
    proj_weight = w_qkv[0].reshape(model_width, -1)
    local_cols = w_out.shape[1]
    quad_cols = model_width // QUAD
    gain_rows = q_gain[0]
    head_count, head_size = gain_rows.shape
    shift_row = mod_shift[0]
    scale_row = mod_scale[0]
    gate_row = mod_gate[0]
    patch_rows = stale_kv.shape[2]
    place = seq_index % QUAD
    out_weights = []
    for offset in range(QUAD):
        piece = lax.dynamic_slice_in_dim(w_out[0], (place ^ offset) * quad_cols, quad_cols, 1)
        if offset:
            piece = permute_seq(piece, lambda i, k=offset: i ^ k)
        out_weights.append(piece)
    norms = call(
        functools.partial(stale_kernel, head_size=head_size),
        [jax.ShapeDtypeStruct((patch_count, patch_rows, local_cols), jnp.bfloat16)],
        (stale_kv[0, :, :, 0],),
    )[0]
    values = stale_kv[0, :, :, 1]
    kv_state = jnp.zeros_like(stale_kv[0])
    produced = jnp.zeros((patch_count, shard_rows, model_width), jnp.bfloat16)
    slot_ids = jnp.arange(patch_count, dtype=jnp.int32)
    carried = None
    for wave_index in range(patch_count):
        position = jnp.mod(wave_index - section_index, patch_count)
        patch_index = jnp.sum(jnp.where(slot_ids == position, patch_order, 0))
        incoming = lax.dynamic_index_in_dim(latent, patch_index, 0, keepdims=False)
        if wave_index == 0:
            incoming = jnp.where(section_index == 0, incoming, in_flight[0])
        hidden = incoming
        if wave_index > 0:
            sections = lax.axis_size("section")
            arrived = lax.ppermute(carried, "section", [(i, i + 1) for i in range(sections - 1)])
            hidden = jnp.where(section_index == 0, hidden, arrived)
        normed = modulate(hidden, shift_row, scale_row)
        pieces = [piece for pair in gather_tokens(normed) for piece in pair]
        place_now = jnp.stack([patch_index, seq_index // 2, seq_index % 2]).astype(jnp.int32)
        state = jax.ShapeDtypeStruct(norms.shape, jnp.bfloat16)
        mixed = jax.ShapeDtypeStruct((patch_rows, local_cols), jnp.bfloat16)
        blended, fresh_key, norms, values = call(
            functools.partial(
                block_kernel, head_size=head_size, shard_rows=shard_rows, query_rows=128
            ),
            [mixed, mixed, state, state],
            (
                place_now,
                jnp.concatenate(pieces, axis=0),
                proj_weight,
                gain_rows.reshape(1, local_cols),
                norms,
                values,
            ),
            scratch=[pltpu.VMEM((patch_rows, 3 * local_cols), jnp.float32)],
            scalars=1,
            flops=2 * patch_rows * model_width * 3 * local_cols,
        )
        fresh_value = lax.dynamic_index_in_dim(values, patch_index, 0, keepdims=False)
        kv_state = lax.dynamic_update_index_in_dim(
            kv_state, jnp.stack([fresh_key, fresh_value], axis=1), patch_index, 0
        )
        others = [blended] + [
            permute_seq(blended, lambda i, k=offset: i ^ k) for offset in range(1, QUAD)
        ]
        (partial,) = call(
            out_kernel,
            [jax.ShapeDtypeStruct((patch_rows, quad_cols), jnp.bfloat16)],
            (*others, *out_weights),
            flops=2 * patch_rows * local_cols * model_width,
        )
        terms = lax.all_to_all(
            partial.reshape(seq_size, shard_rows, quad_cols), "seq", 0, 0, tiled=True
        )
        (result,) = call(
            join_kernel,
            [jax.ShapeDtypeStruct(hidden.shape, jnp.bfloat16)],
            (terms, hidden, gate_row[None]),
        )
        carried = result
        produced = lax.dynamic_update_index_in_dim(produced, result, patch_index, 0)
    return (produced[None], kv_state[None])


def solution(mesh):
    placed = (
        P(None, "seq", None),
        P("section", "seq", None),
        P(),
        P("section", None, None, "seq"),
        P("section", "seq", None),
        P("section", None, None, None, "seq"),
        P("section", None),
        P("section", None),
        P("section", None),
        P("section", "seq", None),
    )
    return jax.shard_map(
        shards,
        mesh=mesh,
        in_specs=placed,
        out_specs=(P("section", None, "seq", None), P("section", None, None, None, "seq")),
        check_vma=False,
    )
```

```python
import functools
import math

import jax
import jax.numpy as jnp
from jax import lax
from jax.experimental import pallas as pl
from jax.experimental.pallas import tpu as pltpu
from jax.sharding import PartitionSpec as P

QUAD = 4
VMEM = pl.BlockSpec(memory_space=pltpu.VMEM)
SMEM = pl.BlockSpec(memory_space=pltpu.SMEM)
LIMIT = 24 * 1024 * 1024


def call(kernel, outs, operands, scratch=(), flops=0, aliases=None, scalars=2, resident=True):
    bytes_accessed = sum(v.size * v.dtype.itemsize for v in operands)
    operands = [
        v
        if at < scalars or not resident
        else pltpu.with_memory_space_constraint(v, pltpu.VMEM)
        for at, v in enumerate(operands)
    ]
    return pl.pallas_call(
        kernel,
        out_shape=[pltpu.VMEM(shape, dtype) for shape, dtype in outs],
        in_specs=[SMEM] * scalars + [VMEM] * (len(operands) - scalars),
        out_specs=[VMEM] * len(outs),
        scratch_shapes=list(scratch),
        input_output_aliases=aliases or {},
        compiler_params=pltpu.CompilerParams(vmem_limit_bytes=LIMIT),
        cost_estimate=pl.CostEstimate(
            flops=flops, bytes_accessed=bytes_accessed, transcendentals=0
        ),
    )(*operands)


def permute_seq(values, target):
    peers = lax.axis_size("seq")
    return lax.ppermute(values, "seq", [(i, target(i) % peers) for i in range(peers)])


def moved(values, along, across=0):
    return permute_seq(values, lambda i: (i + 2 * along) ^ across)


def head_norms(values, head_size):
    normed = []
    for start in range(0, values.shape[1], head_size):
        head = values[:, start : start + head_size]
        mean = jnp.mean(head * head, axis=-1, keepdims=True)
        normed.append(head * lax.rsqrt(mean + 1e-06))
    return jnp.concatenate(normed, axis=1)


def patch_of(spot_ref, order_ref, wave_index):
    count = order_ref.shape[0]
    position = lax.rem(lax.rem(wave_index - spot_ref[0], count) + count, count)
    return order_ref[position]


def modulate_kernel(
    spot_ref,
    order_ref,
    latent_ref,
    arrived_ref,
    shift_ref,
    scale_ref,
    hidden_ref,
    out_ref,
    *,
    wave_index,
):
    patch = patch_of(spot_ref, order_ref, wave_index)
    hidden = jnp.where(
        spot_ref[0] == 0,
        latent_ref[patch].astype(jnp.float32),
        arrived_ref[...].astype(jnp.float32),
    )
    hidden_ref[...] = hidden.astype(jnp.bfloat16)
    centred = hidden - jnp.mean(hidden, axis=-1, keepdims=True)
    spread = jnp.mean(centred * centred, axis=-1, keepdims=True)
    out_ref[...] = (
        centred * lax.rsqrt(spread + 1e-06) * (1.0 + scale_ref[...]) + shift_ref[...]
    ).astype(jnp.bfloat16)


def stale_kernel(keys_ref, norms_ref, raw_ref, *, head_size):
    for slot in range(keys_ref.shape[0]):
        keys = keys_ref[slot]
        raw_ref[slot] = keys
        norms_ref[slot] = head_norms(keys.astype(jnp.float32), head_size).astype(jnp.bfloat16)


def deal_kernel(spot_ref, weight_ref, after_ref, *out_refs, offsets):
    width = out_refs[0].shape[1]
    place = lax.rem(spot_ref[1], QUAD)
    for offset, out_ref in zip(offsets, out_refs):
        start = pl.multiple_of((place ^ offset) * width, 128)
        out_ref[...] = weight_ref[:, pl.ds(start, width)]


def project(spot_ref, pieces, weight_ref, gain_ref, staged_ref, tokens_ref, blocks, head_size):
    shard_rows = pieces[0].shape[0]
    cols = gain_ref.shape[1]
    half = staged_ref.shape[0] // shard_rows // 2
    for at in range(0, len(pieces), 2):
        pair = [pieces[at][...].astype(jnp.float32), pieces[at + 1][...].astype(jnp.float32)]
        tokens_ref[at * shard_rows : (at + 2) * shard_rows] = jnp.concatenate(
            pair, axis=0
        ).astype(jnp.bfloat16)
    fold = math.log2(math.e) / math.sqrt(head_size)
    products = [
        jnp.dot(tokens_ref[...], weight_ref[part], preferred_element_type=jnp.float32)
        for part in range(3)
    ]
    key = products[1].astype(jnp.bfloat16).astype(jnp.float32)
    results = [
        head_norms(products[0], head_size) * (gain_ref[...] * fold),
        key,
        head_norms(key, head_size),
        products[2],
    ]
    depth = lax.div(spot_ref[1], 2)
    column = lax.rem(spot_ref[1], 2)
    for at, (behind, across) in enumerate(blocks):
        line = lax.rem(depth - behind + half, half)
        block = 2 * line + (1 - column if across else column)
        rows = pl.ds(pl.multiple_of(block * shard_rows, 8), shard_rows)
        for part, result in enumerate(results):
            staged_ref[rows, part * cols : (part + 1) * cols] = result[
                at * shard_rows : (at + 1) * shard_rows
            ]


def early_kernel(*refs, blocks, head_size):
    count = len(blocks)
    spot_ref, pieces, weight_ref, gain_ref = refs[0], refs[2 : 2 + count], refs[2 + count], refs[3 + count]
    staged_ref, tokens_ref = refs[-2], refs[-1]
    project(spot_ref, pieces, weight_ref, gain_ref, staged_ref, tokens_ref, blocks, head_size)


def block_kernel(*refs, blocks, head_size, query_rows, wave_index):
    count = len(blocks)
    spot_ref, pieces, weight_ref, gain_ref = refs[0], refs[2 : 2 + count], refs[2 + count], refs[3 + count]
    mixed_ref, staged_ref, norms_ref, raw_ref, values_ref, tokens_ref = refs[-6:]
    slots, rows, cols = norms_ref.shape
    project(spot_ref, pieces, weight_ref, gain_ref, staged_ref, tokens_ref, blocks, head_size)
    slot = patch_of(spot_ref, refs[1], wave_index)
    raw_ref[slot] = staged_ref[:, cols : 2 * cols].astype(jnp.bfloat16)
    norms_ref[slot] = staged_ref[:, 2 * cols : 3 * cols].astype(jnp.bfloat16)
    values_ref[slot] = staged_ref[:, 3 * cols :].astype(jnp.bfloat16)
    for start in range(0, cols, head_size):
        head_cols = slice(start, start + head_size)
        keys = norms_ref[:, :, head_cols].reshape(slots * rows, head_size)
        values = values_ref[:, :, head_cols].reshape(slots * rows, head_size)
        for first in range(0, rows, query_rows):
            here = slice(first, first + query_rows)
            scores = lax.dot_general(
                staged_ref[here, head_cols].astype(jnp.bfloat16),
                keys,
                (((1,), (1,)), ((), ())),
                preferred_element_type=jnp.float32,
            )
            exponent = jnp.exp2(scores)
            total = jnp.sum(exponent, axis=-1, keepdims=True)
            mixed = jnp.dot(
                exponent.astype(jnp.bfloat16), values, preferred_element_type=jnp.float32
            )
            mixed_ref[here, head_cols] = (mixed / total).astype(jnp.bfloat16)


def out_kernel(*refs):
    pieces, weights, out_ref = refs[: len(refs) // 2], refs[len(refs) // 2 : -1], refs[-1]
    total = None
    for piece, weight in zip(pieces, weights):
        term = jnp.dot(piece[...], weight[...], preferred_element_type=jnp.float32)
        total = term if total is None else total + term
    out_ref[...] = total.astype(jnp.bfloat16)


def join_kernel(terms_ref, hidden_ref, gate_ref, out_ref):
    senders, rows, width = terms_ref.shape
    for place in range(QUAD):
        cols = slice(place * width, (place + 1) * width)
        total = None
        for first in range(0, senders, QUAD):
            term = terms_ref[first + place].astype(jnp.float32)
            total = term if total is None else total + term
        out_ref[:, cols] = (
            hidden_ref[:, cols].astype(jnp.float32) + gate_ref[:, cols] * total
        ).astype(jnp.bfloat16)


def finish_kernel(spot_ref, order_ref, terms_ref, hidden_ref, gate_ref, *refs):
    earlier, out_ref = refs[:-1], refs[-1]
    for wave_index, result in enumerate(earlier):
        out_ref[patch_of(spot_ref, order_ref, wave_index)] = result[...]
    last = patch_of(spot_ref, order_ref, len(earlier))
    join_kernel(terms_ref, hidden_ref, gate_ref, out_ref.at[last])


def shards(
    latent, in_flight, patch_order, w_qkv, w_out, stale_kv, mod_shift, mod_scale, mod_gate, q_gain
):
    bf16, f32 = jnp.bfloat16, jnp.float32
    patch_count, shard_rows, model_width = latent.shape
    section_index = lax.axis_index("section")
    seq_index = lax.axis_index("seq")
    seq_size = lax.axis_size("seq")
    local_cols = w_out.shape[1]
    quad_cols = model_width // QUAD
    head_size = q_gain.shape[2]
    patch_rows = stale_kv.shape[2]
    gain = q_gain[0].reshape(1, local_cols)
    weight = jnp.transpose(w_qkv[0], (1, 0, 2))
    state = ((patch_count, patch_rows, local_cols), bf16)
    hidden_type = ((shard_rows, model_width), bf16)
    spot = jnp.stack([section_index, seq_index]).astype(jnp.int32)
    norms, raw = call(
        functools.partial(stale_kernel, head_size=head_size),
        [state, state],
        (stale_kv[0, :, :, 0],),
        scalars=0,
    )
    values = stale_kv[0, :, :, 1]
    arrived = in_flight[0]
    results = []
    out_weights = []

    def deal(offsets, after):
        pieces = call(
            functools.partial(deal_kernel, offsets=offsets),
            [((local_cols, quad_cols), bf16)] * len(offsets),
            (spot, w_out[0], after),
            scalars=1,
        )
        for offset, piece in zip(offsets, pieces):
            out_weights.append(
                permute_seq(piece, lambda i: i ^ offset) if offset else piece
            )

    for wave_index in range(patch_count):
        if wave_index > 0:
            sections = lax.axis_size("section")
            arrived = lax.ppermute(
                results[-1], "section", [(i, i + 1) for i in range(sections - 1)]
            )
        hidden, own = call(
            functools.partial(modulate_kernel, wave_index=wave_index),
            [hidden_type, hidden_type],
            (spot, patch_order, latent, arrived, mod_shift, mod_scale),
            resident=wave_index > 0,
        )
        got = {(0, 0): own}
        for key, along, across in ((1, 1, 0), (-1, -1, 0), (2, 2, 0), (-2, -2, 0)):
            got[key, 0] = moved(own, along, across)
        got[0, 1] = moved(own, 0, 1)
        if wave_index == 0:
            deal((0, 1), own)
        got[3, 0] = moved(got[2, 0], 1)
        got[-3, 0] = moved(got[-2, 0], -1)
        got[1, 1] = moved(got[0, 1], 1)
        got[-1, 1] = moved(got[0, 1], -1)
        got[2, 1] = moved(got[2, 0], 0, 1)
        got[-2, 1] = moved(got[-2, 0], 0, 1)
        if wave_index == 0:
            deal((2,), got[2, 0])
            deal((3,), got[3, 0])
        got[4, 0] = moved(got[3, 0], 1)
        got[4, 1] = moved(got[-3, 0], -1, 1)
        got[3, 1] = moved(got[2, 1], 1)
        got[-3, 1] = moved(got[-2, 1], -1)
        groups = [
            [(0, 0), (0, 1), (1, 0), (-1, 0), (2, 0), (-2, 0)],
            [(1, 1), (-1, 1), (3, 0), (-3, 0), (2, 1), (-2, 1)],
            [(4, 0), (4, 1), (3, 1), (-3, 1)],
        ]
        staged_type = ((patch_rows, 4 * local_cols), f32)
        staged = ()
        for group in groups[:2]:
            staged = call(
                functools.partial(early_kernel, blocks=group, head_size=head_size),
                [staged_type],
                (spot, patch_order, *[got[key] for key in group], weight, gain, *staged),
                scratch=[pltpu.VMEM((len(group) * shard_rows, model_width), bf16)],
                flops=6 * len(group) * shard_rows * model_width * local_cols,
                aliases={len(group) + 4: 0} if staged else None,
            )
        group = groups[2]
        blended, _, norms, raw, values = call(
            functools.partial(
                block_kernel,
                blocks=group,
                head_size=head_size,
                query_rows=patch_rows // 2,
                wave_index=wave_index,
            ),
            [((patch_rows, local_cols), bf16), staged_type, state, state, state],
            (
                spot,
                patch_order,
                *[got[key] for key in group],
                weight,
                gain,
                *staged,
                norms,
                raw,
                values,
            ),
            scratch=[pltpu.VMEM((len(group) * shard_rows, model_width), bf16)],
            flops=6 * patch_rows * model_width * local_cols,
            aliases={len(group) + 4 + at: 1 + at for at in range(4)},
        )
        others = [blended] + [
            permute_seq(blended, lambda i, k=offset: i ^ k) for offset in range(1, QUAD)
        ]
        (partial,) = call(
            out_kernel,
            [((patch_rows, quad_cols), bf16)],
            (*others, *out_weights),
            scalars=0,
            flops=2 * patch_rows * local_cols * model_width,
        )
        terms = lax.all_to_all(
            partial.reshape(seq_size, shard_rows, quad_cols), "seq", 0, 0, tiled=True
        )
        if wave_index + 1 < patch_count:
            results += call(join_kernel, [hidden_type], (terms, hidden, mod_gate), scalars=0)
    (produced,) = call(
        finish_kernel,
        [((patch_count, shard_rows, model_width), bf16)],
        (spot, patch_order, terms, hidden, mod_gate, *results),
    )
    return (produced[None], jnp.stack([raw, values], axis=2)[None])


def solution(mesh):
    placed = (
        P(None, "seq", None),
        P("section", "seq", None),
        P(),
        P("section", None, None, "seq"),
        P("section", "seq", None),
        P("section", None, None, None, "seq"),
        P("section", None),
        P("section", None),
        P("section", None),
        P("section", "seq", None),
    )
    return jax.shard_map(
        shards,
        mesh=mesh,
        in_specs=placed,
        out_specs=(P("section", None, "seq", None), P("section", None, None, None, "seq")),
        check_vma=False,
    )
```

```python
import functools
import math

import jax
import jax.numpy as jnp
from jax import lax
from jax.experimental import pallas as pl
from jax.experimental.pallas import tpu as pltpu
from jax.sharding import PartitionSpec as P

QUAD = 4
VMEM = pl.BlockSpec(memory_space=pltpu.VMEM)
SMEM = pl.BlockSpec(memory_space=pltpu.SMEM)
LIMIT = 24 * 1024 * 1024


HBM = pl.BlockSpec(memory_space=pltpu.HBM)


def call(kernel, outs, operands, scratch=(), flops=0, aliases=None, scalars=2, stay=()):
    bytes_accessed = sum(v.size * v.dtype.itemsize for v in operands)
    operands = [
        v
        if at < scalars
        else pltpu.with_memory_space_constraint(v, pltpu.HBM if at in stay else pltpu.VMEM)
        for at, v in enumerate(operands)
    ]
    return pl.pallas_call(
        kernel,
        out_shape=[pltpu.VMEM(shape, dtype) for shape, dtype in outs],
        in_specs=[
            SMEM if at < scalars else HBM if at in stay else VMEM for at in range(len(operands))
        ],
        out_specs=[VMEM] * len(outs),
        scratch_shapes=list(scratch),
        input_output_aliases=aliases or {},
        compiler_params=pltpu.CompilerParams(vmem_limit_bytes=LIMIT),
        cost_estimate=pl.CostEstimate(
            flops=flops, bytes_accessed=bytes_accessed, transcendentals=0
        ),
    )(*operands)


def permute_seq(values, target):
    peers = lax.axis_size("seq")
    return lax.ppermute(values, "seq", [(i, target(i) % peers) for i in range(peers)])


def moved(values, along, across=0):
    return permute_seq(values, lambda i: (i + 2 * along) ^ across)


def head_norms(values, head_size):
    normed = []
    for start in range(0, values.shape[1], head_size):
        head = values[:, start : start + head_size]
        mean = jnp.mean(head * head, axis=-1, keepdims=True)
        normed.append(head * lax.rsqrt(mean + 1e-06))
    return jnp.concatenate(normed, axis=1)


def patch_of(spot_ref, order_ref, wave_index):
    count = order_ref.shape[0]
    position = lax.rem(lax.rem(wave_index - spot_ref[0], count) + count, count)
    return order_ref[position]


def modulated(hidden, shift, scale):
    centred = hidden - jnp.mean(hidden, axis=-1, keepdims=True)
    spread = jnp.mean(centred * centred, axis=-1, keepdims=True)
    return (centred * lax.rsqrt(spread + 1e-06) * (1.0 + scale) + shift).astype(jnp.bfloat16)


def first_kernel(
    spot_ref,
    order_ref,
    latent_ref,
    given_ref,
    shift_ref,
    scale_ref,
    hidden_ref,
    out_ref,
    rows_ref,
    params_ref,
    sems,
):
    patch = patch_of(spot_ref, order_ref, 0)
    moves = [
        (latent_ref.at[patch], rows_ref.at[0]),
        (given_ref.at[0], rows_ref.at[1]),
        (shift_ref, params_ref.at[0]),
        (scale_ref, params_ref.at[1]),
    ]
    copies = [
        pltpu.make_async_copy(source, target, sems.at[at])
        for at, (source, target) in enumerate(moves)
    ]
    for copy in copies:
        copy.start()
    for copy in copies:
        copy.wait()
    rows = rows_ref[jnp.where(spot_ref[0] == 0, 0, 1)]
    hidden_ref[...] = rows
    out_ref[...] = modulated(rows.astype(jnp.float32), params_ref[0], params_ref[1])


def modulate_kernel(*refs):
    count = len(refs) // 2 - 1
    shift_ref, scale_ref = refs[count : count + 2]
    for hidden_ref, out_ref in zip(refs[:count], refs[count + 2 :]):
        out_ref[...] = modulated(
            hidden_ref[...].astype(jnp.float32), shift_ref[...], scale_ref[...]
        )


def stale_kernel(keys_ref, norms_ref, raw_ref, *, head_size):
    for slot in range(keys_ref.shape[0]):
        keys = keys_ref[slot]
        raw_ref[slot] = keys
        norms_ref[slot] = head_norms(keys.astype(jnp.float32), head_size).astype(jnp.bfloat16)


def deal_kernel(spot_ref, weight_ref, after_ref, *out_refs, offsets):
    width = out_refs[0].shape[1]
    place = lax.rem(spot_ref[1], QUAD)
    for offset, out_ref in zip(offsets, out_refs):
        start = pl.multiple_of((place ^ offset) * width, 128)
        out_ref[...] = weight_ref[:, pl.ds(start, width)]


def project(spot_ref, pieces, weight_ref, gain_ref, staged_ref, tokens_ref, blocks, head_size):
    shard_rows = pieces[0].shape[0]
    cols = gain_ref.shape[1]
    half = staged_ref.shape[0] // shard_rows // 2
    for at in range(0, len(pieces), 2):
        pair = [pieces[at][...].astype(jnp.float32), pieces[at + 1][...].astype(jnp.float32)]
        tokens_ref[at * shard_rows : (at + 2) * shard_rows] = jnp.concatenate(
            pair, axis=0
        ).astype(jnp.bfloat16)
    fold = math.log2(math.e) / math.sqrt(head_size)
    products = [
        jnp.dot(tokens_ref[...], weight_ref[part], preferred_element_type=jnp.float32)
        for part in range(3)
    ]
    key = products[1].astype(jnp.bfloat16).astype(jnp.float32)
    results = [
        head_norms(products[0], head_size) * (gain_ref[...] * fold),
        key,
        head_norms(key, head_size),
        products[2],
    ]
    depth = lax.div(spot_ref[1], 2)
    column = lax.rem(spot_ref[1], 2)
    for at, (behind, across) in enumerate(blocks):
        line = lax.rem(depth - behind + half, half)
        block = 2 * line + (1 - column if across else column)
        rows = pl.ds(pl.multiple_of(block * shard_rows, 8), shard_rows)
        for part, result in enumerate(results):
            staged_ref[rows, part * cols : (part + 1) * cols] = result[
                at * shard_rows : (at + 1) * shard_rows
            ]


def early_kernel(*refs, blocks, head_size):
    count = len(blocks)
    spot_ref, pieces, weight_ref, gain_ref = refs[0], refs[2 : 2 + count], refs[2 + count], refs[3 + count]
    staged_ref, tokens_ref = refs[-2], refs[-1]
    project(spot_ref, pieces, weight_ref, gain_ref, staged_ref, tokens_ref, blocks, head_size)


def block_kernel(*refs, blocks, head_size, query_rows, wave_index):
    count = len(blocks)
    spot_ref, pieces, weight_ref, gain_ref = refs[0], refs[2 : 2 + count], refs[2 + count], refs[3 + count]
    mixed_ref, staged_ref, norms_ref, raw_ref, values_ref, tokens_ref = refs[-6:]
    slots, rows, cols = norms_ref.shape
    project(spot_ref, pieces, weight_ref, gain_ref, staged_ref, tokens_ref, blocks, head_size)
    slot = patch_of(spot_ref, refs[1], wave_index)
    raw_ref[slot] = staged_ref[:, cols : 2 * cols].astype(jnp.bfloat16)
    norms_ref[slot] = staged_ref[:, 2 * cols : 3 * cols].astype(jnp.bfloat16)
    values_ref[slot] = staged_ref[:, 3 * cols :].astype(jnp.bfloat16)
    for start in range(0, cols, head_size):
        head_cols = slice(start, start + head_size)
        keys = norms_ref[:, :, head_cols].reshape(slots * rows, head_size)
        values = values_ref[:, :, head_cols].reshape(slots * rows, head_size)
        for first in range(0, rows, query_rows):
            here = slice(first, first + query_rows)
            scores = lax.dot_general(
                staged_ref[here, head_cols].astype(jnp.bfloat16),
                keys,
                (((1,), (1,)), ((), ())),
                preferred_element_type=jnp.float32,
            )
            exponent = jnp.exp2(scores)
            total = jnp.sum(exponent, axis=-1, keepdims=True)
            mixed = jnp.dot(
                exponent.astype(jnp.bfloat16), values, preferred_element_type=jnp.float32
            )
            mixed_ref[here, head_cols] = (mixed / total).astype(jnp.bfloat16)


def out_kernel(*refs):
    pieces, weights, out_ref = refs[:QUAD], refs[QUAD : 2 * QUAD], refs[-1]
    total = None
    for piece, weight in zip(pieces, weights):
        term = jnp.dot(piece[...], weight[...], preferred_element_type=jnp.float32)
        total = term if total is None else total + term
    out_ref[...] = total.astype(jnp.bfloat16)


def join(terms_ref, hidden_ref, gate_ref, out_ref):
    senders, rows, width = terms_ref.shape
    for place in range(QUAD):
        cols = slice(place * width, (place + 1) * width)
        total = None
        for first in range(0, senders, QUAD):
            term = terms_ref[first + place].astype(jnp.float32)
            total = term if total is None else total + term
        out_ref[:, cols] = (
            hidden_ref[:, cols].astype(jnp.float32) + gate_ref[:, cols] * total
        ).astype(jnp.bfloat16)


def join_kernel(
    spot_ref,
    order_ref,
    terms_ref,
    hidden_ref,
    gate_ref,
    latent_ref,
    out_ref,
    send_ref,
    *,
    wave_index,
    sections,
):
    join(terms_ref, hidden_ref, gate_ref, out_ref)
    count = order_ref.shape[0]
    rows = latent_ref[order_ref[(wave_index + 1) % count]]
    send_ref[...] = jnp.where(
        spot_ref[0] == sections - 1, rows.astype(jnp.float32), out_ref[...].astype(jnp.float32)
    ).astype(jnp.bfloat16)


def finish_kernel(spot_ref, order_ref, terms_ref, hidden_ref, gate_ref, *refs):
    earlier, out_ref = refs[:-1], refs[-1]
    for wave_index, result in enumerate(earlier):
        out_ref[patch_of(spot_ref, order_ref, wave_index)] = result[...]
    last = patch_of(spot_ref, order_ref, len(earlier))
    join(terms_ref, hidden_ref, gate_ref, out_ref.at[last])


def shards(
    latent, in_flight, patch_order, w_qkv, w_out, stale_kv, mod_shift, mod_scale, mod_gate, q_gain
):
    bf16, f32 = jnp.bfloat16, jnp.float32
    patch_count, shard_rows, model_width = latent.shape
    section_index = lax.axis_index("section")
    seq_index = lax.axis_index("seq")
    seq_size = lax.axis_size("seq")
    local_cols = w_out.shape[1]
    quad_cols = model_width // QUAD
    head_size = q_gain.shape[2]
    patch_rows = stale_kv.shape[2]
    gain = q_gain[0].reshape(1, local_cols)
    weight = jnp.transpose(w_qkv[0], (1, 0, 2))
    state = ((patch_count, patch_rows, local_cols), bf16)
    hidden_type = ((shard_rows, model_width), bf16)
    spot = jnp.stack([section_index, seq_index]).astype(jnp.int32)
    norms, raw = call(
        functools.partial(stale_kernel, head_size=head_size),
        [state, state],
        (stale_kv[0, :, :, 0],),
        scalars=0,
    )
    values = stale_kv[0, :, :, 1]
    results = []
    out_weights = []

    def deal(offsets, after):
        pieces = call(
            functools.partial(deal_kernel, offsets=offsets),
            [((local_cols, quad_cols), bf16)] * len(offsets),
            (spot, w_out[0], after),
            scalars=1,
        )
        for offset, piece in zip(offsets, pieces):
            out_weights.append(
                permute_seq(piece, lambda i: i ^ offset) if offset else piece
            )

    sections = lax.axis_size("section")

    def forward(rows, along, across):
        pairs = [
            (
                section * seq_size + i,
                (section + 1) % sections * seq_size + ((i + 2 * along) ^ across) % seq_size,
            )
            for section in range(sections)
            for i in range(seq_size)
        ]
        return lax.ppermute(rows, ("section", "seq"), pairs)

    for wave_index in range(patch_count):
        base = 0 if wave_index == 0 else 1
        if wave_index == 0:
            hidden, own = call(
                first_kernel,
                [hidden_type, hidden_type],
                (spot, patch_order, latent, in_flight, mod_shift, mod_scale),
                scratch=[
                    pltpu.VMEM((2, shard_rows, model_width), bf16),
                    pltpu.VMEM((2, 1, model_width), f32),
                    pltpu.SemaphoreType.DMA((4,)),
                ],
                stay=(2, 3, 4, 5),
            )
            normed = [own]
        else:
            near = [forward(sent, along, 1) for along in (0, 1, -1)] + [forward(sent, 0, 0)]
            hidden = near[3]
            normed = call(
                modulate_kernel,
                [hidden_type] * len(near),
                (*near, mod_shift, mod_scale),
                scalars=0,
            )
        start = [(0, base), (1, base), (-1, base), (0, 1 - base)]
        got = dict(zip(start, normed))
        if wave_index == 0:
            for sign in (1, -1):
                got[sign, 0] = moved(got[0, 0], sign)
                got[2 * sign, 0] = moved(got[0, 0], 2 * sign)
            got[0, 1] = moved(got[0, 0], 0, 1)
            deal((0, 1), got[0, 0])
            for sign in (1, -1):
                got[3 * sign, 0] = moved(got[2 * sign, 0], sign)
                got[sign, 1] = moved(got[0, 1], sign)
                got[2 * sign, 1] = moved(got[2 * sign, 0], 0, 1)
            deal((2,), got[2, 0])
            deal((3,), got[3, 0])
            for sign in (1, -1):
                got[3 * sign, 1] = moved(got[2 * sign, 1], sign)
            groups = [
                start + [(2, 0), (-2, 0)],
                [(1, 1), (-1, 1), (3, 0), (-3, 0), (2, 1), (-2, 1)],
                [(4, 0), (4, 1), (3, 1), (-3, 1)],
            ]
        else:
            for sign in (1, -1):
                got[2 * sign, base] = moved(got[sign, base], sign)
                got[3 * sign, base] = moved(got[sign, base], 2 * sign)
                got[sign, 1 - base] = moved(got[sign, base], 0, 1)
            for sign in (1, -1):
                got[2 * sign, 1 - base] = moved(got[sign, 1 - base], sign)
                got[3 * sign, 1 - base] = moved(got[3 * sign, base], 0, 1)
            groups = [
                start,
                [(at, base) for at in (2, -2, 3, -3)] + [(at, 1 - base) for at in (1, -1)],
                [(4, base), (4, 1 - base)] + [(at, 1 - base) for at in (2, -2, 3, -3)],
            ]
        got[4, base] = moved(got[3, base], 1)
        got[4, 1 - base] = moved(got[-3, base], -1, 1)
        staged_type = ((patch_rows, 4 * local_cols), f32)
        staged = ()
        for group in groups[:2]:
            staged = call(
                functools.partial(early_kernel, blocks=group, head_size=head_size),
                [staged_type],
                (spot, patch_order, *[got[key] for key in group], weight, gain, *staged),
                scratch=[pltpu.VMEM((len(group) * shard_rows, model_width), bf16)],
                flops=6 * len(group) * shard_rows * model_width * local_cols,
                aliases={len(group) + 4: 0} if staged else None,
            )
        group = groups[2]
        blended, _, norms, raw, values = call(
            functools.partial(
                block_kernel,
                blocks=group,
                head_size=head_size,
                query_rows=patch_rows // 2,
                wave_index=wave_index,
            ),
            [((patch_rows, local_cols), bf16), staged_type, state, state, state],
            (
                spot,
                patch_order,
                *[got[key] for key in group],
                weight,
                gain,
                *staged,
                norms,
                raw,
                values,
            ),
            scratch=[pltpu.VMEM((len(group) * shard_rows, model_width), bf16)],
            flops=6 * patch_rows * model_width * local_cols,
            aliases={len(group) + 4 + at: 1 + at for at in range(4)},
        )
        others = [blended] + [
            permute_seq(blended, lambda i, k=offset: i ^ k) for offset in range(1, QUAD)
        ]
        (partial,) = call(
            out_kernel,
            [((patch_rows, quad_cols), bf16)],
            (*others, *out_weights),
            scalars=0,
            flops=2 * patch_rows * local_cols * model_width,
        )
        terms = lax.all_to_all(
            partial.reshape(seq_size, shard_rows, quad_cols), "seq", 0, 0, tiled=True
        )
        if wave_index + 1 < patch_count:
            result, sent = call(
                functools.partial(join_kernel, wave_index=wave_index, sections=sections),
                [hidden_type, hidden_type],
                (spot, patch_order, terms, hidden, mod_gate, latent),
            )
            results.append(result)
    (produced,) = call(
        finish_kernel,
        [((patch_count, shard_rows, model_width), bf16)],
        (spot, patch_order, terms, hidden, mod_gate, *results),
    )
    return (produced[None], jnp.stack([raw, values], axis=2)[None])


def solution(mesh):
    placed = (
        P(None, "seq", None),
        P("section", "seq", None),
        P(),
        P("section", None, None, "seq"),
        P("section", "seq", None),
        P("section", None, None, None, "seq"),
        P("section", None),
        P("section", None),
        P("section", None),
        P("section", "seq", None),
    )
    return jax.shard_map(
        shards,
        mesh=mesh,
        in_specs=placed,
        out_specs=(P("section", None, "seq", None), P("section", None, None, None, "seq")),
        check_vma=False,
    )
```

```python
import functools
import math

import jax
import jax.numpy as jnp
from jax import lax
from jax.experimental import pallas as pl
from jax.experimental.pallas import tpu as pltpu
from jax.sharding import PartitionSpec as P

QUAD = 4
VMEM = pl.BlockSpec(memory_space=pltpu.VMEM)
SMEM = pl.BlockSpec(memory_space=pltpu.SMEM)
LIMIT = 24 * 1024 * 1024


HBM = pl.BlockSpec(memory_space=pltpu.HBM)


def call(
    kernel, outs, operands, scratch=(), flops=0, aliases=None, scalars=2, stay=(), kept=True
):
    bytes_accessed = sum(v.size * v.dtype.itemsize for v in operands)
    operands = [
        v
        if at < scalars
        else pltpu.with_memory_space_constraint(v, pltpu.HBM if at in stay else pltpu.VMEM)
        for at, v in enumerate(operands)
    ]
    return pl.pallas_call(
        kernel,
        out_shape=[
            pltpu.VMEM(shape, dtype) if kept else jax.ShapeDtypeStruct(shape, dtype)
            for shape, dtype in outs
        ],
        in_specs=[
            SMEM if at < scalars else HBM if at in stay else VMEM for at in range(len(operands))
        ],
        out_specs=[VMEM] * len(outs),
        scratch_shapes=list(scratch),
        input_output_aliases=aliases or {},
        compiler_params=pltpu.CompilerParams(vmem_limit_bytes=LIMIT),
        cost_estimate=pl.CostEstimate(
            flops=flops, bytes_accessed=bytes_accessed, transcendentals=0
        ),
    )(*operands)


def permute_seq(values, target):
    peers = lax.axis_size("seq")
    return lax.ppermute(values, "seq", [(i, target(i) % peers) for i in range(peers)])


def moved(values, along, across=0):
    return permute_seq(values, lambda i: (i + 2 * along) ^ across)


def head_norms(values, head_size):
    normed = []
    for start in range(0, values.shape[1], head_size):
        head = values[:, start : start + head_size]
        mean = jnp.mean(head * head, axis=-1, keepdims=True)
        normed.append(head * lax.rsqrt(mean + 1e-06))
    return jnp.concatenate(normed, axis=1)


def patch_of(spot_ref, order_ref, wave_index):
    count = order_ref.shape[0]
    position = lax.rem(lax.rem(wave_index - spot_ref[0], count) + count, count)
    return order_ref[position]


def modulated(hidden, shift, scale):
    centred = hidden - jnp.mean(hidden, axis=-1, keepdims=True)
    spread = jnp.mean(centred * centred, axis=-1, keepdims=True)
    return (centred * lax.rsqrt(spread + 1e-06) * (1.0 + scale) + shift).astype(jnp.bfloat16)


def first_kernel(
    spot_ref,
    order_ref,
    latent_ref,
    given_ref,
    shift_ref,
    scale_ref,
    hidden_ref,
    out_ref,
    rows_ref,
    params_ref,
    sems,
):
    patch = patch_of(spot_ref, order_ref, 0)
    moves = [
        (latent_ref.at[patch], rows_ref.at[0]),
        (given_ref.at[0], rows_ref.at[1]),
        (shift_ref, params_ref.at[0]),
        (scale_ref, params_ref.at[1]),
    ]
    copies = [
        pltpu.make_async_copy(source, target, sems.at[at])
        for at, (source, target) in enumerate(moves)
    ]
    for copy in copies:
        copy.start()
    for copy in copies:
        copy.wait()
    rows = rows_ref[jnp.where(spot_ref[0] == 0, 0, 1)]
    hidden_ref[...] = rows
    out_ref[...] = modulated(rows.astype(jnp.float32), params_ref[0], params_ref[1])


def modulate_kernel(*refs):
    count = len(refs) // 2 - 1
    shift_ref, scale_ref = refs[count : count + 2]
    for hidden_ref, out_ref in zip(refs[:count], refs[count + 2 :]):
        out_ref[...] = modulated(
            hidden_ref[...].astype(jnp.float32), shift_ref[...], scale_ref[...]
        )


def stale_kernel(keys_ref, norms_ref, raw_ref, *, head_size):
    for slot in range(keys_ref.shape[0]):
        keys = keys_ref[slot]
        raw_ref[slot] = keys
        norms_ref[slot] = head_norms(keys.astype(jnp.float32), head_size).astype(jnp.bfloat16)


def deal_kernel(spot_ref, weight_ref, after_ref, *out_refs, offsets):
    width = out_refs[0].shape[1]
    place = lax.rem(spot_ref[1], QUAD)
    for offset, out_ref in zip(offsets, out_refs):
        start = pl.multiple_of((place ^ offset) * width, 128)
        out_ref[...] = weight_ref[:, pl.ds(start, width)]


def project(spot_ref, pieces, weight_ref, gain_ref, staged_ref, tokens_ref, blocks, head_size):
    shard_rows = pieces[0].shape[0]
    cols = gain_ref.shape[1]
    half = staged_ref.shape[0] // shard_rows // 2
    for at in range(0, len(pieces), 2):
        pair = [pieces[at][...].astype(jnp.float32), pieces[at + 1][...].astype(jnp.float32)]
        tokens_ref[at * shard_rows : (at + 2) * shard_rows] = jnp.concatenate(
            pair, axis=0
        ).astype(jnp.bfloat16)
    fold = math.log2(math.e) / math.sqrt(head_size)
    products = [
        jnp.dot(tokens_ref[...], weight_ref[part], preferred_element_type=jnp.float32)
        for part in range(3)
    ]
    key = products[1].astype(jnp.bfloat16).astype(jnp.float32)
    results = [
        head_norms(products[0], head_size) * (gain_ref[...] * fold),
        key,
        head_norms(key, head_size),
        products[2],
    ]
    depth = lax.div(spot_ref[1], 2)
    column = lax.rem(spot_ref[1], 2)
    for at, (behind, across) in enumerate(blocks):
        line = lax.rem(depth - behind + half, half)
        block = 2 * line + (1 - column if across else column)
        rows = pl.ds(pl.multiple_of(block * shard_rows, 8), shard_rows)
        for part, result in enumerate(results):
            staged_ref[rows, part * cols : (part + 1) * cols] = result[
                at * shard_rows : (at + 1) * shard_rows
            ]


def early_kernel(*refs, blocks, head_size):
    count = len(blocks)
    spot_ref, pieces, weight_ref, gain_ref = refs[0], refs[2 : 2 + count], refs[2 + count], refs[3 + count]
    staged_ref, tokens_ref = refs[-2], refs[-1]
    project(spot_ref, pieces, weight_ref, gain_ref, staged_ref, tokens_ref, blocks, head_size)


def block_kernel(*refs, blocks, head_size, query_rows, wave_index):
    count = len(blocks)
    spot_ref, pieces, weight_ref, gain_ref = refs[0], refs[2 : 2 + count], refs[2 + count], refs[3 + count]
    mixed_ref, staged_ref, norms_ref, raw_ref, values_ref, tokens_ref = refs[-6:]
    slots, rows, cols = norms_ref.shape
    project(spot_ref, pieces, weight_ref, gain_ref, staged_ref, tokens_ref, blocks, head_size)
    slot = patch_of(spot_ref, refs[1], wave_index)
    raw_ref[slot] = staged_ref[:, cols : 2 * cols].astype(jnp.bfloat16)
    norms_ref[slot] = staged_ref[:, 2 * cols : 3 * cols].astype(jnp.bfloat16)
    values_ref[slot] = staged_ref[:, 3 * cols :].astype(jnp.bfloat16)
    for start in range(0, cols, head_size):
        head_cols = slice(start, start + head_size)
        keys = norms_ref[:, :, head_cols].reshape(slots * rows, head_size)
        values = values_ref[:, :, head_cols].reshape(slots * rows, head_size)
        for first in range(0, rows, query_rows):
            here = slice(first, first + query_rows)
            scores = lax.dot_general(
                staged_ref[here, head_cols].astype(jnp.bfloat16),
                keys,
                (((1,), (1,)), ((), ())),
                preferred_element_type=jnp.float32,
            )
            exponent = jnp.exp2(scores)
            total = jnp.sum(exponent, axis=-1, keepdims=True)
            mixed = jnp.dot(
                exponent.astype(jnp.bfloat16), values, preferred_element_type=jnp.float32
            )
            mixed_ref[here, head_cols] = (mixed / total).astype(jnp.bfloat16)


def out_kernel(*refs):
    pieces, weights, out_ref = refs[:QUAD], refs[QUAD : 2 * QUAD], refs[-1]
    total = None
    for piece, weight in zip(pieces, weights):
        term = jnp.dot(piece[...], weight[...], preferred_element_type=jnp.float32)
        total = term if total is None else total + term
    out_ref[...] = total.astype(jnp.bfloat16)


def join(terms_ref, hidden_ref, gate_ref, out_ref):
    senders, rows, width = terms_ref.shape
    for place in range(QUAD):
        cols = slice(place * width, (place + 1) * width)
        total = None
        for first in range(0, senders, QUAD):
            term = terms_ref[first + place].astype(jnp.float32)
            total = term if total is None else total + term
        out_ref[:, cols] = (
            hidden_ref[:, cols].astype(jnp.float32) + gate_ref[:, cols] * total
        ).astype(jnp.bfloat16)


def join_kernel(
    spot_ref,
    order_ref,
    terms_ref,
    hidden_ref,
    gate_ref,
    latent_ref,
    out_ref,
    send_ref,
    *,
    wave_index,
    sections,
):
    join(terms_ref, hidden_ref, gate_ref, out_ref)
    count = order_ref.shape[0]
    rows = latent_ref[order_ref[(wave_index + 1) % count]]
    send_ref[...] = jnp.where(
        spot_ref[0] == sections - 1, rows.astype(jnp.float32), out_ref[...].astype(jnp.float32)
    ).astype(jnp.bfloat16)


def finish_kernel(spot_ref, order_ref, terms_ref, hidden_ref, gate_ref, *refs):
    earlier, out_ref = refs[:-1], refs[-1]
    for wave_index, result in enumerate(earlier):
        out_ref[patch_of(spot_ref, order_ref, wave_index)] = result[...]
    last = patch_of(spot_ref, order_ref, len(earlier))
    join(terms_ref, hidden_ref, gate_ref, out_ref.at[last])


def shards(
    latent, in_flight, patch_order, w_qkv, w_out, stale_kv, mod_shift, mod_scale, mod_gate, q_gain
):
    bf16, f32 = jnp.bfloat16, jnp.float32
    patch_count, shard_rows, model_width = latent.shape
    section_index = lax.axis_index("section")
    seq_index = lax.axis_index("seq")
    seq_size = lax.axis_size("seq")
    local_cols = w_out.shape[1]
    quad_cols = model_width // QUAD
    head_size = q_gain.shape[2]
    patch_rows = stale_kv.shape[2]
    gain = q_gain[0].reshape(1, local_cols)
    weight = jnp.transpose(w_qkv[0], (1, 0, 2))
    state = ((patch_count, patch_rows, local_cols), bf16)
    hidden_type = ((shard_rows, model_width), bf16)
    spot = jnp.stack([section_index, seq_index]).astype(jnp.int32)
    norms, raw = call(
        functools.partial(stale_kernel, head_size=head_size),
        [state, state],
        (stale_kv[0, :, :, 0],),
        scalars=0,
    )
    values = stale_kv[0, :, :, 1]
    results = []
    out_weights = []

    def deal(offsets, after):
        pieces = call(
            functools.partial(deal_kernel, offsets=offsets),
            [((local_cols, quad_cols), bf16)] * len(offsets),
            (spot, w_out[0], after),
            scalars=1,
        )
        for offset, piece in zip(offsets, pieces):
            out_weights.append(
                permute_seq(piece, lambda i: i ^ offset) if offset else piece
            )

    sections = lax.axis_size("section")

    def forward(rows, along, across):
        pairs = [
            (
                section * seq_size + i,
                (section + 1) % sections * seq_size + ((i + 2 * along) ^ across) % seq_size,
            )
            for section in range(sections)
            for i in range(seq_size)
        ]
        return lax.ppermute(rows, ("section", "seq"), pairs)

    for wave_index in range(patch_count):
        base = 0 if wave_index == 0 else 1
        if wave_index == 0:
            hidden, own = call(
                first_kernel,
                [hidden_type, hidden_type],
                (spot, patch_order, latent, in_flight, mod_shift, mod_scale),
                scratch=[
                    pltpu.VMEM((2, shard_rows, model_width), bf16),
                    pltpu.VMEM((2, 1, model_width), f32),
                    pltpu.SemaphoreType.DMA((4,)),
                ],
                stay=(2, 3, 4, 5),
            )
            normed = [own]
        else:
            near = [forward(sent, along, 1) for along in (0, 1, -1)] + [forward(sent, 0, 0)]
            hidden = near[3]
            normed = call(
                modulate_kernel,
                [hidden_type] * len(near),
                (*near, mod_shift, mod_scale),
                scalars=0,
            )
        start = [(0, base), (1, base), (-1, base), (0, 1 - base)]
        got = dict(zip(start, normed))
        if wave_index == 0:
            for sign in (1, -1):
                got[sign, 0] = moved(got[0, 0], sign)
                got[2 * sign, 0] = moved(got[0, 0], 2 * sign)
            got[0, 1] = moved(got[0, 0], 0, 1)
            deal((0, 1), got[0, 0])
            for sign in (1, -1):
                got[3 * sign, 0] = moved(got[2 * sign, 0], sign)
                got[sign, 1] = moved(got[0, 1], sign)
                got[2 * sign, 1] = moved(got[2 * sign, 0], 0, 1)
            deal((2,), got[2, 0])
            deal((3,), got[3, 0])
            for sign in (1, -1):
                got[3 * sign, 1] = moved(got[2 * sign, 1], sign)
            groups = [
                start + [(2, 0), (-2, 0)],
                [(1, 1), (-1, 1), (3, 0), (-3, 0), (2, 1), (-2, 1)],
                [(4, 0), (4, 1), (3, 1), (-3, 1)],
            ]
        else:
            for sign in (1, -1):
                got[2 * sign, base] = moved(got[sign, base], sign)
                got[3 * sign, base] = moved(got[sign, base], 2 * sign)
                got[sign, 1 - base] = moved(got[sign, base], 0, 1)
            for sign in (1, -1):
                got[2 * sign, 1 - base] = moved(got[sign, 1 - base], sign)
                got[3 * sign, 1 - base] = moved(got[3 * sign, base], 0, 1)
            groups = [
                start,
                [(at, base) for at in (2, -2, 3, -3)] + [(at, 1 - base) for at in (1, -1)],
                [(4, base), (4, 1 - base)] + [(at, 1 - base) for at in (2, -2, 3, -3)],
            ]
        got[4, base] = moved(got[3, base], 1)
        got[4, 1 - base] = moved(got[-3, base], -1, 1)
        staged_type = ((patch_rows, 4 * local_cols), f32)
        staged = ()
        for group in groups[:2]:
            staged = call(
                functools.partial(early_kernel, blocks=group, head_size=head_size),
                [staged_type],
                (spot, patch_order, *[got[key] for key in group], weight, gain, *staged),
                scratch=[pltpu.VMEM((len(group) * shard_rows, model_width), bf16)],
                flops=6 * len(group) * shard_rows * model_width * local_cols,
                aliases={len(group) + 4: 0} if staged else None,
            )
        group = groups[2]
        blended, _, norms, raw, values = call(
            functools.partial(
                block_kernel,
                blocks=group,
                head_size=head_size,
                query_rows=patch_rows // 2,
                wave_index=wave_index,
            ),
            [((patch_rows, local_cols), bf16), staged_type, state, state, state],
            (
                spot,
                patch_order,
                *[got[key] for key in group],
                weight,
                gain,
                *staged,
                norms,
                raw,
                values,
            ),
            scratch=[pltpu.VMEM((len(group) * shard_rows, model_width), bf16)],
            flops=6 * patch_rows * model_width * local_cols,
            aliases={len(group) + 4 + at: 1 + at for at in range(4)},
        )
        others = [blended] + [
            permute_seq(blended, lambda i, k=offset: i ^ k) for offset in range(1, QUAD)
        ]
        (partial,) = call(
            out_kernel,
            [((patch_rows, quad_cols), bf16)],
            (*others, *out_weights),
            scalars=0,
            flops=2 * patch_rows * local_cols * model_width,
        )
        terms = lax.all_to_all(
            partial.reshape(seq_size, shard_rows, quad_cols), "seq", 0, 0, tiled=True
        )
        if wave_index + 1 < patch_count:
            result, sent = call(
                functools.partial(join_kernel, wave_index=wave_index, sections=sections),
                [hidden_type, hidden_type],
                (spot, patch_order, terms, hidden, mod_gate, latent),
            )
            results.append(result)
    (produced,) = call(
        finish_kernel,
        [((patch_count, shard_rows, model_width), bf16)],
        (spot, patch_order, terms, hidden, mod_gate, *results),
        kept=False,
    )
    return (produced[None], jnp.stack([raw, values], axis=2)[None])


def solution(mesh):
    placed = (
        P(None, "seq", None),
        P("section", "seq", None),
        P(),
        P("section", None, None, "seq"),
        P("section", "seq", None),
        P("section", None, None, None, "seq"),
        P("section", None),
        P("section", None),
        P("section", None),
        P("section", "seq", None),
    )
    return jax.shard_map(
        shards,
        mesh=mesh,
        in_specs=placed,
        out_specs=(P("section", None, "seq", None), P("section", None, None, None, "seq")),
        check_vma=False,
    )
```
